256 devices in a mesh: dom: 32 (over x, z), space: 8 (over y, core).
Axes of the slice: x: 4, y: 4, z: 8, core: 2. Of those that a mesh axis runs over, the one named last changes fastest.
Arguments:
- particles: float32 [512, 3, 128, 512], P('dom', None, 'space'), as said below
- counts: int32 [512], P('dom'), may hold values from 0 to 2, as said below
- bathymetry: float32 [128, 512], P('space'), may hold values from -0.5 to 0.5
Outputs:
- advanced: float32 [512, 3, 128, 512], P('dom', None, 'space')
The draws below stay inside these ranges and needn't reach their ends.
Inputs may be any that keep to these rules, and one draw needn't show every extreme that they name: The counts sum to 512; counts[p] + counts[p + 256] = 2 for every p below 256; the particles of one group have at most 32 offspring together, and some group has exactly that many. `particles`: depths stay between 0.55 and 1.45, momenta within 0.6.
All inputs are finite; a program needn't handle non-finite values.
Results may differ from the reference program's by a relative error of at most 0.00002.
Values sent between devices are 32-bit elements; how exact they have to be, the bound alone decides.
No kernel may reach another device: no remote copies, remote signals or barrier semaphores. Data moves between devices by JAX's collectives and lax.ppermute only.
A program may use at most 64 MiB of HBM per device.

```python
import jax
import jax.numpy as jnp
from jax import lax

PART_DEV = 16
COLS = 512
PARTICLES = 512
ROWS = 128
N_DOM = 32


def draw_particles(key, part):
    key = jax.random.fold_in(key, 2)
    first_key, second_key = jax.random.split(key, 2)
    depth = 1.0 + 0.3 * jnp.clip(jax.random.normal(first_key, (PARTICLES, 1, ROWS, COLS), jnp.float32), -1.5, 1.5)
    flow = 0.15 * jnp.clip(jax.random.normal(second_key, (PARTICLES, 2, ROWS, COLS), jnp.float32), -4.0, 4.0)
    return jnp.concatenate([depth, flow], axis=1).astype(jnp.float32)


def draw_counts(key, part):
    key = jax.random.fold_in(key, 1)
    half = PARTICLES // 2
    kinds = jax.random.randint(key, (half,), 0, 3)
    members = jnp.arange(half, dtype=jnp.int32)
    kinds = jnp.where(members < PART_DEV, 1, kinds)
    lower = jnp.where(kinds == 0, 1, jnp.where(kinds == 1, 2, 0))
    upper = 2 - lower
    return jnp.concatenate([lower, upper]).astype(jnp.int32)


def block_scale(own_key, extent, cuts, smallest, largest):
    gain = 1.0
    for axis_at, parts in cuts:
        heights = jax.random.uniform(jax.random.fold_in(jax.random.fold_in(own_key, 6), axis_at), (parts,), jnp.float32, smallest / len(cuts), largest / len(cuts))
        gain = gain * jnp.repeat(jnp.exp(heights), extent[axis_at] // parts).reshape((-1,) + (1,) * (len(extent) - 1 - axis_at))
    return gain


def setup_inputs(seed: int = 0) -> dict:
    key_of = jax.random.split(jax.random.key(seed), 4)
    particles = draw_particles(jax.random.fold_in(key_of[3], 71), 0)
    counts = draw_counts(jax.random.fold_in(key_of[3], 71), 0)
    bathymetry = jnp.clip(jax.random.uniform(key_of[2], (ROWS, COLS), jnp.float32, -0.5, 0.5) * block_scale(key_of[2], (ROWS, COLS), ((0, 8),), -0.4, 0.0), -0.5, 0.5)
    return {"particles": particles, "counts": counts, "bathymetry": bathymetry}


GRAVITY = 1.0
RATIO = 0.25


def advance(padded, bed):
    depth = padded[:, 0]
    east_flow = padded[:, 1]
    north_flow = padded[:, 2]
    flux_x = jnp.stack([east_flow, east_flow * east_flow / depth + 0.5 * GRAVITY * depth * depth, east_flow * north_flow / depth], 1)
    flux_y = jnp.stack([north_flow, east_flow * north_flow / depth, north_flow * north_flow / depth + 0.5 * GRAVITY * depth * depth], 1)
    centre = padded[:, :, 1:-1]
    inner_x = flux_x[:, :, 1:-1]
    mean = (jnp.roll(centre, -1, -1) + jnp.roll(centre, 1, -1) + padded[:, :, 2:] + padded[:, :, :-2]) * 0.25
    drift = mean - 0.5 * RATIO * (jnp.roll(inner_x, -1, -1) - jnp.roll(inner_x, 1, -1)) - 0.5 * RATIO * (flux_y[:, :, 2:] - flux_y[:, :, :-2])
    middle_depth = depth[:, 1:-1]
    bed_mid = bed[1:-1]
    slope_x = 0.5 * (jnp.roll(bed_mid, -1, -1) - jnp.roll(bed_mid, 1, -1))
    slope_y = 0.5 * (bed[2:] - bed[:-2])
    source = jnp.stack([jnp.zeros_like(middle_depth), -RATIO * GRAVITY * middle_depth * slope_x, -RATIO * GRAVITY * middle_depth * slope_y], 1)
    return drift + source


def reference(particles, counts, bathymetry):
    ends = jnp.cumsum(counts).astype(jnp.int32)
    places = jnp.arange(PARTICLES, dtype=jnp.int32)
    slots = ((places % PART_DEV) * N_DOM + places // PART_DEV).astype(jnp.int32)
    source = jnp.sum((ends[None, :] <= slots[:, None]).astype(jnp.int32), axis=1).astype(jnp.int32)
    chosen = jnp.take(particles, source, axis=0)
    bed = jnp.concatenate([bathymetry[-1:], bathymetry, bathymetry[:1]], axis=0)

    def one(state):
        state = state[None]
        for turn in range(2):
            padded = jnp.concatenate([state[:, :, -1:], state, state[:, :, :1]], axis=2)
            state = advance(padded, bed)
        return state[0]

    return lax.map(one, chosen)
```

```python
import jax
import jax.numpy as jnp
from jax import lax
from jax.experimental import pallas as pl
from jax.experimental.pallas import tpu as pltpu
from jax.sharding import PartitionSpec as P


def halo_permutes(particles, bed):
    count = lax.axis_size("space")
    rows = particles.shape[2]
    up = [(i, (i + 1) % count) for i in range(count)]
    down = [(target, source) for source, target in up]
    flat = particles.reshape((-1,) + particles.shape[2:])

    def edge(lo):
        return jnp.concatenate([flat[:, lo : lo + 2], bed[None, lo : lo + 2]], axis=0)

    low = lax.ppermute(edge(rows - 2), "space", up)
    high = lax.ppermute(edge(0), "space", down)
    return low, high


def one_step(h, m, n, slope_x, slope_y):
    rows, cols = h.shape
    inv = 1.0 / h
    u = m * inv
    press = 0.0625 * (h * h)
    fx = 0.125 * (m * u) + press
    cross = 0.125 * (u * n)
    gy = 0.125 * (n * (n * inv)) + press

    def combine(q, f, g):
        q = 0.25 * q
        return (
            pltpu.roll(q - f, cols - 1, 1)
            + pltpu.roll(q + f, 1, 1)
            + pltpu.roll(q - g, rows - 1, 0)
            + pltpu.roll(q + g, 1, 0)
        )

    return (
        combine(h, 0.125 * m, 0.125 * n),
        combine(m, fx, cross) + h * slope_x,
        combine(n, cross, gy) + h * slope_y,
    )


def evolve_kernel(x_ref, low_ref, high_ref, bed_ref, bed_low_ref, bed_high_ref, o_ref, ext, sx, sy):
    rows = x_ref.shape[2]
    cols = x_ref.shape[3]

    @pl.when(pl.program_id(0) == 0)
    def _():
        ext[...] = jnp.ones_like(ext)
        ext[0, 0:rows] = bed_ref[...]
        ext[0, rows : rows + 2] = bed_high_ref[0]
        ext[0, rows + 6 : rows + 8] = bed_low_ref[0]
        b = ext[0]
        sx[...] = -0.125 * (pltpu.roll(b, cols - 1, 1) - pltpu.roll(b, 1, 1))
        sy[...] = -0.125 * (pltpu.roll(b, rows + 7, 0) - pltpu.roll(b, 1, 0))

    for f in range(3):
        ext[f, 0:rows] = x_ref[0, f]
        ext[f, rows : rows + 2] = high_ref[f]
        ext[f, rows + 6 : rows + 8] = low_ref[f]
    slope_x = sx[...]
    slope_y = sy[...]
    state = (ext[0], ext[1], ext[2])
    for _ in range(2):
        state = one_step(*state, slope_x, slope_y)
    for f in range(3):
        o_ref[0, f] = state[f][0:rows]


def evolve(particles, bed, low, high):
    count, fields, rows, cols = particles.shape
    return pl.pallas_call(
        evolve_kernel,
        grid=(count,),
        in_specs=[
            pl.BlockSpec((1, fields, rows, cols), lambda i: (i, 0, 0, 0)),
            pl.BlockSpec((fields, 2, cols), lambda i: (i, 0, 0)),
            pl.BlockSpec((fields, 2, cols), lambda i: (i, 0, 0)),
            pl.BlockSpec((rows, cols), lambda i: (0, 0)),
            pl.BlockSpec((1, 2, cols), lambda i: (count * fields, 0, 0)),
            pl.BlockSpec((1, 2, cols), lambda i: (count * fields, 0, 0)),
        ],
        out_specs=pl.BlockSpec((1, fields, rows, cols), lambda i: (i, 0, 0, 0)),
        out_shape=jax.ShapeDtypeStruct(particles.shape, jnp.float32),
        scratch_shapes=[
            pltpu.VMEM((fields, rows + 8, cols), jnp.float32),
            pltpu.VMEM((rows + 8, cols), jnp.float32),
            pltpu.VMEM((rows + 8, cols), jnp.float32),
        ],
    )(particles, low, high, bed, low, high)


def per_device(particles, counts, bed):
    groups = lax.axis_size("dom")
    per_group = counts.shape[0]
    me = lax.axis_index("dom")
    low, high = halo_permutes(particles, bed)
    total = jnp.sum(counts)
    totals = lax.all_to_all(
        jnp.broadcast_to(total[None], (groups,)), "dom", 0, 0, tiled=True
    )
    index = jnp.arange(groups, dtype=jnp.int32)
    ends = jnp.sum(jnp.where(index[None, :] <= index[:, None], totals[None, :], 0), axis=1)
    base = jnp.sum(jnp.where(index < me, totals, 0))
    done = evolve(particles, bed, low, high)
    local_ends = jnp.cumsum(counts)
    offset = (index - base) % groups
    source = jnp.sum((local_ends[None, :] <= offset[:, None]).astype(jnp.int32), axis=1)
    parcel = jnp.take(done, jnp.minimum(source, per_group - 1), axis=0, mode="clip")
    parcel = lax.all_to_all(parcel, "dom", 0, 0, tiled=True)
    wanted = jnp.arange(per_group, dtype=jnp.int32) * groups + me
    entry = jnp.sum((ends[None, :] <= wanted[:, None]).astype(jnp.int32), axis=1)
    return jnp.take(parcel, entry, axis=0, mode="clip")


def solution(mesh):
    in_specs = (P("dom", None, "space", None), P("dom"), P("space", None))
    out_specs = P("dom", None, "space", None)
    return jax.shard_map(
        per_device, mesh=mesh, in_specs=in_specs, out_specs=out_specs, check_vma=False
    )
```

```python
import functools

import jax
import jax.numpy as jnp
from jax import lax
from jax.experimental import pallas as pl
from jax.experimental.pallas import tpu as pltpu
from jax.sharding import Mesh, PartitionSpec as P

F32 = jnp.float32
XS, ZS = 4, 8
LANES = 128
BOXES = 10
VMEM = pl.BlockSpec(memory_space=pltpu.VMEM)
SMEM = pl.BlockSpec(memory_space=pltpu.SMEM)


def one_step(h, m, n, slope_x, slope_y):
    rows, cols = h.shape
    inv = 1.0 / h
    u = m * inv
    press = 0.0625 * (h * h)
    fx = 0.125 * (m * u) + press
    cross = 0.125 * (u * n)
    gy = 0.125 * (n * (n * inv)) + press

    def combine(q, f, g):
        q = 0.25 * q
        return (
            pltpu.roll(q - f, cols - 1, 1)
            + pltpu.roll(q + f, 1, 1)
            + pltpu.roll(q - g, rows - 1, 0)
            + pltpu.roll(q + g, 1, 0)
        )

    return (
        combine(h, 0.125 * m, 0.125 * n),
        combine(m, fx, cross) + h * slope_x,
        combine(n, cross, gy) + h * slope_y,
    )


def edge_kernel(place_ref, x_ref, bed_ref, counts_ref, low_ref, high_ref, row_ref):
    count, fields, rows, _ = x_ref.shape
    for p in range(count):
        for f in range(fields):
            low_ref[p * fields + f] = x_ref[p, f, rows - 2 : rows]
            high_ref[p * fields + f] = x_ref[p, f, 0:2]
    low_ref[count * fields] = bed_ref[rows - 2 : rows]
    high_ref[count * fields] = bed_ref[0:2]
    sub = lax.broadcasted_iota(jnp.int32, (8, LANES), 0)
    lane = lax.broadcasted_iota(jnp.int32, (8, LANES), 1)
    total = jnp.int32(0)
    tile = jnp.zeros((8, LANES), jnp.int32)
    for j in range(count):
        c = counts_ref[j]
        total = total + c
        tile = jnp.where(lane == j, c, tile)
    tile = jnp.where(lane == count, total, tile)
    tile = jnp.where(sub == place_ref[1], tile, 0).astype(F32)
    for z in range(ZS):
        row_ref[z] = tile


def evolve_kernel(place_ref, x_ref, low_ref, high_ref, bed_ref, row_ref, *refs):
    upper, lower = refs[0:XS], refs[XS : 2 * XS]
    ext, sx, sy, res = refs[2 * XS :]
    count, fields, rows, cols = x_ref.shape
    ext[...] = jnp.ones_like(ext)
    ext[0, 0:rows] = bed_ref[...]
    ext[0, rows : rows + 2] = high_ref[count * fields]
    ext[0, rows + 6 : rows + 8] = low_ref[count * fields]
    b = ext[0]
    sx[...] = -0.125 * (pltpu.roll(b, cols - 1, 1) - pltpu.roll(b, 1, 1))
    sy[...] = -0.125 * (pltpu.roll(b, rows + 7, 0) - pltpu.roll(b, 1, 0))
    x = place_ref[0]

    def body(p, carry):
        for f in range(fields):
            ext[f, 0:rows] = x_ref[p, f]
            ext[f, rows : rows + 2] = high_ref[p * fields + f]
            ext[f, rows + 6 : rows + 8] = low_ref[p * fields + f]
        slope_x = sx[...]
        slope_y = sy[...]
        state = (ext[0], ext[1], ext[2])
        for _ in range(2):
            state = one_step(*state, slope_x, slope_y)
        for f in range(fields):
            res[f] = state[f][0:rows]
        for k in range(XS):
            at = pl.multiple_of(((x + k) % XS) * LANES, LANES)
            for f in range(fields):
                upper[k][p, f] = res[f, 0:8, pl.ds(at, LANES)]
                lower[k][p, f] = res[f, 8:16, pl.ds(at, LANES)]
        return carry

    lax.fori_loop(0, count, body, 0)
    tile = row_ref[0]
    for z in range(1, ZS):
        tile = tile + row_ref[z]
    for k in range(XS):
        upper[k][count, 0] = tile
        upper[k][count, 1] = tile
        upper[k][count, 2] = tile


def load_counts(x, tiles, cnt, sem):
    copies = []
    for k in range(XS):
        copies.append(
            pltpu.make_async_copy(tiles[k], cnt.at[(x + XS - k) % XS], sem.at[k])
        )
    for copy in copies:
        copy.start()
    for copy in copies:
        copy.wait()


def pack_kernel(with_table, half, place_ref, *refs):
    tiles, data = refs[0:XS], refs[XS : 2 * XS]
    out_ref = refs[2 * XS]
    table_ref = refs[2 * XS + 1] if with_table else None
    cnt, base, ctr, sem = refs[-4:]
    x, z = place_ref[0], place_ref[1]
    load_counts(x, [t.at[16, 0] for t in tiles], cnt, sem)
    total = jnp.int32(0)
    for g in range(XS * ZS):
        base[g] = total
        total = total + cnt[g // ZS, g % ZS, 16].astype(jnp.int32)
    base[XS * ZS] = total
    for i in range(ZS):
        ctr[i] = 0

    def put(src, j, slot):
        to = slot & (ZS - 1)
        t = ctr[to]
        ctr[to] = t + 1
        out_ref[to, t] = src[j]

    for k in range(XS):
        at = (x + XS - k) % XS
        src = data[k]

        def body(j, e):
            c = cnt[at, z, j].astype(jnp.int32)

            @pl.when(c > 0)
            def _():
                put(src, j, e)

            @pl.when(c > 1)
            def _():
                put(src, j, e + 1)

            return e + c

        lax.fori_loop(0, 16, body, base[at * ZS + z])

    if with_table:
        for i in range(ZS):
            ctr[i] = 0
        for i in range(16 * XS):
            table_ref[i] = 0
        for k in range(XS):
            at = (x + XS - k) % XS

            def groups(zs, carry):
                lo = base[at * ZS + zs]
                hi = base[at * ZS + zs + 1]
                first = lo + ((z - lo) & (ZS - 1))
                for i in range(4):
                    s = first + i * ZS

                    @pl.when(s < hi)
                    def _():
                        t = ctr[zs]
                        ctr[zs] = t + 1
                        table_ref[s >> 3] = zs * 16 + t

                return carry

            lax.fori_loop(0, ZS, groups, 0)


def pack(place, tiles, data, with_table):
    out_shape = [jax.ShapeDtypeStruct((ZS, BOXES, 3, 8, LANES), F32)]
    out_specs = [VMEM]
    if with_table:
        out_shape.append(jax.ShapeDtypeStruct((16 * XS,), jnp.int32))
        out_specs.append(SMEM)
    return pl.pallas_call(
        functools.partial(pack_kernel, with_table, 0),
        in_specs=[SMEM] + [VMEM] * (2 * XS),
        out_specs=out_specs,
        out_shape=out_shape,
        scratch_shapes=[
            pltpu.SMEM((XS, 8, LANES), F32),
            pltpu.SMEM((XS * ZS + 1,), jnp.int32),
            pltpu.SMEM((ZS,), jnp.int32),
            pltpu.SemaphoreType.DMA((XS,)),
        ],
        cost_estimate=pl.CostEstimate(flops=0, bytes_accessed=4_000_000, transcendentals=0),
    )(place, *tiles, *data)


def spread_kernel(place_ref, table_ref, in_ref, *outs):
    x = place_ref[0]
    for k in range(XS):
        to = (x + k) % XS
        out = outs[k]

        def body(i, carry):
            code = table_ref[i * XS + to]
            out[i] = in_ref[code >> 4, code & 15]
            return carry

        lax.fori_loop(0, 16, body, 0, unroll=4)


def spread(place, table, boxes):
    return pl.pallas_call(
        spread_kernel,
        in_specs=[SMEM, SMEM, VMEM],
        out_specs=[VMEM] * XS,
        out_shape=[jax.ShapeDtypeStruct((16, 3, 8, LANES), F32)] * XS,
        cost_estimate=pl.CostEstimate(flops=0, bytes_accessed=4_000_000, transcendentals=0),
    )(place, table, boxes)


def join_kernel(place_ref, *refs):
    parts, out_ref = refs[: 2 * XS], refs[2 * XS]
    x = place_ref[0]
    for k in range(XS):
        at = pl.multiple_of(((x + XS - k) % XS) * LANES, LANES)

        def body(i, carry):
            for f in range(3):
                out_ref[i, f, 0:8, pl.ds(at, LANES)] = parts[k][i, f]
                out_ref[i, f, 8:16, pl.ds(at, LANES)] = parts[XS + k][i, f]
            return carry

        lax.fori_loop(0, 16, body, 0, unroll=4)


def along_x(parts):
    return [parts[0]] + [
        lax.ppermute(parts[k], "x", [(i, (i + k) % XS) for i in range(XS)]) for k in range(1, XS)
    ]


def per_device(particles, counts, bed):
    count, fields, rows, cols = particles.shape
    place = jnp.stack([lax.axis_index("x"), lax.axis_index("z")]).astype(jnp.int32)
    edges = jax.ShapeDtypeStruct((count * fields + 1, 2, cols), F32)
    low, high, row = pl.pallas_call(
        edge_kernel,
        in_specs=[SMEM, VMEM, VMEM, SMEM],
        out_specs=[VMEM] * 3,
        out_shape=[edges, edges, jax.ShapeDtypeStruct((ZS, 8, LANES), F32)],
    )(place, particles, bed, counts)
    strips = lax.axis_size("space")
    low = lax.ppermute(low, "space", [(i, (i + 1) % strips) for i in range(strips)])
    high = lax.ppermute(high, "space", [((i + 1) % strips, i) for i in range(strips)])
    row = lax.all_to_all(row, "z", 0, 0, tiled=True)
    first = jax.ShapeDtypeStruct((count + 1, fields, 8, LANES), F32)
    second = jax.ShapeDtypeStruct((count, fields, 8, LANES), F32)
    parts = pl.pallas_call(
        evolve_kernel,
        in_specs=[SMEM] + [VMEM] * 5,
        out_specs=[VMEM] * (2 * XS),
        out_shape=[first] * XS + [second] * XS,
        scratch_shapes=[
            pltpu.VMEM((fields, rows + 8, cols), F32),
            pltpu.VMEM((rows + 8, cols), F32),
            pltpu.VMEM((rows + 8, cols), F32),
            pltpu.VMEM((fields, rows, cols), F32),
        ],
        cost_estimate=pl.CostEstimate(flops=0, bytes_accessed=20_000_000, transcendentals=0),
    )(place, particles, low, high, bed, row)
    upper = along_x(parts[:XS])
    lower = along_x(parts[XS:])
    boxes_a, table = pack(place, upper, upper, True)
    boxes_a = lax.all_to_all(boxes_a, "z", 0, 0, tiled=True)
    boxes_b = pack(place, upper, lower, False)[0]
    boxes_b = lax.all_to_all(boxes_b, "z", 0, 0, tiled=True)
    out_a = along_x(spread(place, table, boxes_a))
    out_b = along_x(spread(place, table, boxes_b))
    return pl.pallas_call(
        join_kernel,
        in_specs=[SMEM] + [VMEM] * (2 * XS),
        out_specs=VMEM,
        out_shape=jax.ShapeDtypeStruct(particles.shape, F32),
    )(place, *out_a, *out_b)


def solution(mesh):
    wide = Mesh(mesh.devices.reshape(XS, ZS, -1), ("x", "z", "space"))
    in_specs = (P(("x", "z"), None, "space", None), P(("x", "z")), P("space", None))
    out_specs = P(("x", "z"), None, "space", None)
    return jax.shard_map(
        per_device, mesh=wide, in_specs=in_specs, out_specs=out_specs, check_vma=False
    )
```

```python
import functools

import jax
import jax.numpy as jnp
from jax import lax
from jax.experimental import pallas as pl
from jax.experimental.pallas import tpu as pltpu
from jax.sharding import Mesh, PartitionSpec as P

F32 = jnp.float32
XS, ZS = 4, 8
LANES = 128
BOXES = 10
VMEM = pl.BlockSpec(memory_space=pltpu.VMEM)
SMEM = pl.BlockSpec(memory_space=pltpu.SMEM)
PARAMS = pltpu.CompilerParams(vmem_limit_bytes=12 * 1024 * 1024)


def one_step(h, m, n, slope_x, slope_y):
    rows, cols = h.shape
    inv = 1.0 / h
    u = m * inv
    press = 0.0625 * (h * h)
    fx = 0.125 * (m * u) + press
    cross = 0.125 * (u * n)
    gy = 0.125 * (n * (n * inv)) + press

    def combine(q, f, g):
        q = 0.25 * q
        return (
            pltpu.roll(q - f, cols - 1, 1)
            + pltpu.roll(q + f, 1, 1)
            + pltpu.roll(q - g, rows - 1, 0)
            + pltpu.roll(q + g, 1, 0)
        )

    return (
        combine(h, 0.125 * m, 0.125 * n),
        combine(m, fx, cross) + h * slope_x,
        combine(n, cross, gy) + h * slope_y,
    )


def edge_kernel(x_ref, bed_ref, low_ref, high_ref):
    count, fields, rows, _ = x_ref.shape
    for p in range(count):
        for f in range(fields):
            low_ref[p * fields + f] = x_ref[p, f, rows - 2 : rows]
            high_ref[p * fields + f] = x_ref[p, f, 0:2]
    low_ref[count * fields] = bed_ref[rows - 2 : rows]
    high_ref[count * fields] = bed_ref[0:2]


def evolve_kernel(place_ref, counts_ref, x_ref, low_ref, high_ref, bed_ref, *refs):
    upper, lower = refs[0:XS], refs[XS : 2 * XS]
    row_ref, ext, sx, sy, res = refs[2 * XS :]
    count, fields, rows, cols = x_ref.shape
    ext[...] = jnp.ones_like(ext)
    ext[0, 0:rows] = bed_ref[...]
    ext[0, rows : rows + 2] = high_ref[count * fields]
    ext[0, rows + 6 : rows + 8] = low_ref[count * fields]
    b = ext[0]
    sx[...] = -0.125 * (pltpu.roll(b, cols - 1, 1) - pltpu.roll(b, 1, 1))
    sy[...] = -0.125 * (pltpu.roll(b, rows + 7, 0) - pltpu.roll(b, 1, 0))
    x = place_ref[0]

    def body(p, carry):
        for f in range(fields):
            ext[f, 0:rows] = x_ref[p, f]
            ext[f, rows : rows + 2] = high_ref[p * fields + f]
            ext[f, rows + 6 : rows + 8] = low_ref[p * fields + f]
        slope_x = sx[...]
        slope_y = sy[...]
        state = (ext[0], ext[1], ext[2])
        for _ in range(2):
            state = one_step(*state, slope_x, slope_y)
        for f in range(fields):
            res[f] = state[f][0:rows]
        for k in range(XS):
            at = pl.multiple_of(((x + k) % XS) * LANES, LANES)
            for f in range(fields):
                upper[k][p, f] = res[f, 0:8, pl.ds(at, LANES)]
                lower[k][p, f] = res[f, 8:16, pl.ds(at, LANES)]
        return carry

    lax.fori_loop(0, count, body, 0)
    lane = lax.broadcasted_iota(jnp.int32, (1, LANES), 1)
    total = jnp.int32(0)
    tile = jnp.zeros((1, LANES), jnp.int32)
    for j in range(count):
        c = counts_ref[j]
        total = total + c
        tile = jnp.where(lane == j, c, tile)
    tile = jnp.where(lane == count, total, tile)
    for g in range(XS * ZS):
        row_ref[g] = tile


def plan_kernel(place_ref, row_ref, put_ref, take_ref, base, ctr):
    x, z = place_ref[0], place_ref[1]
    total = jnp.int32(0)
    for g in range(XS * ZS):
        base[g] = total
        total = total + row_ref[g, 0, 16]
    base[XS * ZS] = total
    for i in range(ZS):
        ctr[i] = 0

    def reserve(slot):
        to = slot & (ZS - 1)
        t = ctr[to]
        ctr[to] = t + 1
        return to * 16 + t

    for k in range(XS):
        group = ((x + XS - k) % XS) * ZS + z
        e = base[group]
        for j in range(16):
            c = row_ref[group, 0, j]
            at = 2 * (k * 16 + j)
            put_ref[at] = -1
            put_ref[at + 1] = -1

            @pl.when(c > 0)
            def _():
                put_ref[at] = reserve(e)

            @pl.when(c > 1)
            def _():
                put_ref[at + 1] = reserve(e + 1)

            e = e + c
    spare = jnp.int32(0)
    for i in range(ZS):
        spare = jnp.where(ctr[i] < BOXES, i * 16 + BOXES - 1, spare)
    for i in range(32 * XS):
        code = put_ref[i]
        put_ref[i] = jnp.where(code < 0, spare, code)

    for i in range(ZS):
        ctr[i] = 0
    for i in range(16 * XS):
        take_ref[i] = 0
    for k in range(XS):
        for zs in range(ZS):
            group = ((x + XS - k) % XS) * ZS + zs
            lo = base[group]
            hi = base[group + 1]
            first = lo + ((z - lo) & (ZS - 1))
            t0 = ctr[zs]
            for i in range(4):
                s = first + i * ZS

                @pl.when(s < hi)
                def _():
                    take_ref[s >> 3] = zs * 16 + t0 + i
                    ctr[zs] = t0 + i + 1


def plan(place, row):
    return pl.pallas_call(
        plan_kernel,
        in_specs=[SMEM, SMEM],
        out_specs=[SMEM, SMEM],
        out_shape=[
            jax.ShapeDtypeStruct((32 * XS,), jnp.int32),
            jax.ShapeDtypeStruct((16 * XS,), jnp.int32),
        ],
        scratch_shapes=[
            pltpu.SMEM((XS * ZS + 1,), jnp.int32),
            pltpu.SMEM((ZS,), jnp.int32),
        ],
        compiler_params=PARAMS,
    )(place, row)


def pack_kernel(put_ref, *refs):
    data, out_ref = refs[0:XS], refs[XS]
    for k in range(XS):
        for j in range(16):
            item = data[k][j]
            for i in range(2):
                code = put_ref[2 * (k * 16 + j) + i]
                out_ref[code >> 4, code & 15] = item


def pack(put, data):
    return pl.pallas_call(
        pack_kernel,
        in_specs=[SMEM] + [VMEM] * XS,
        out_specs=VMEM,
        out_shape=jax.ShapeDtypeStruct((ZS, BOXES, 3, 8, LANES), F32),
        compiler_params=PARAMS,
        cost_estimate=pl.CostEstimate(flops=0, bytes_accessed=3_000_000, transcendentals=0),
    )(put, *data)


def spread_kernel(place_ref, table_ref, in_ref, *outs):
    x = place_ref[0]
    for k in range(XS):
        to = (x + k) % XS
        out = outs[k]

        def body(i, carry):
            code = table_ref[i * XS + to]
            out[i] = in_ref[code >> 4, code & 15]
            return carry

        lax.fori_loop(0, 16, body, 0, unroll=4)


def spread(place, table, boxes):
    return pl.pallas_call(
        spread_kernel,
        in_specs=[SMEM, SMEM, VMEM],
        out_specs=[VMEM] * XS,
        out_shape=[jax.ShapeDtypeStruct((16, 3, 8, LANES), F32)] * XS,
        compiler_params=PARAMS,
        cost_estimate=pl.CostEstimate(flops=0, bytes_accessed=4_000_000, transcendentals=0),
    )(place, table, boxes)


def join_kernel(place_ref, *refs):
    parts, out_ref = refs[: 2 * XS], refs[2 * XS]
    x = place_ref[0]
    for k in range(XS):
        at = pl.multiple_of(((x + XS - k) % XS) * LANES, LANES)

        def body(i, carry):
            for f in range(3):
                out_ref[i, f, 0:8, pl.ds(at, LANES)] = parts[k][i, f]
                out_ref[i, f, 8:16, pl.ds(at, LANES)] = parts[XS + k][i, f]
            return carry

        lax.fori_loop(0, 16, body, 0, unroll=4)


def along_x(parts):
    return [parts[0]] + [
        lax.ppermute(parts[k], "x", [(i, (i + k) % XS) for i in range(XS)]) for k in range(1, XS)
    ]


def per_device(particles, counts, bed):
    count, fields, rows, cols = particles.shape
    place = jnp.stack([lax.axis_index("x"), lax.axis_index("z")]).astype(jnp.int32)
    edges = jax.ShapeDtypeStruct((count * fields + 1, 2, cols), F32)
    low, high = pl.pallas_call(
        edge_kernel,
        in_specs=[VMEM, VMEM],
        out_specs=[VMEM] * 2,
        out_shape=[edges, edges],
        compiler_params=PARAMS,
    )(particles, bed)
    strips = lax.axis_size("space")
    low = lax.ppermute(low, "space", [(i, (i + 1) % strips) for i in range(strips)])
    high = lax.ppermute(high, "space", [((i + 1) % strips, i) for i in range(strips)])
    half = jax.ShapeDtypeStruct((count, fields, 8, LANES), F32)
    *parts, row = pl.pallas_call(
        evolve_kernel,
        in_specs=[SMEM, SMEM] + [VMEM] * 4,
        out_specs=[VMEM] * (2 * XS + 1),
        out_shape=[half] * (2 * XS) + [jax.ShapeDtypeStruct((XS * ZS, 1, LANES), jnp.int32)],
        scratch_shapes=[
            pltpu.VMEM((fields, rows + 8, cols), F32),
            pltpu.VMEM((rows + 8, cols), F32),
            pltpu.VMEM((rows + 8, cols), F32),
            pltpu.VMEM((fields, rows, cols), F32),
        ],
        compiler_params=PARAMS,
        cost_estimate=pl.CostEstimate(flops=0, bytes_accessed=20_000_000, transcendentals=0),
    )(place, counts, particles, low, high, bed)
    upper = along_x(parts[:XS])
    row = lax.all_to_all(row, ("x", "z"), 0, 0, tiled=True)
    lower = along_x(parts[XS:])
    put, take = plan(place, row)
    boxes_a = lax.all_to_all(pack(put, upper), "z", 0, 0, tiled=True)
    boxes_b = lax.all_to_all(pack(put, lower), "z", 0, 0, tiled=True)
    out_a = along_x(spread(place, take, boxes_a))
    out_b = along_x(spread(place, take, boxes_b))
    return pl.pallas_call(
        join_kernel,
        in_specs=[SMEM] + [VMEM] * (2 * XS),
        out_specs=VMEM,
        out_shape=jax.ShapeDtypeStruct(particles.shape, F32),
        compiler_params=PARAMS,
    )(place, *out_a, *out_b)


def solution(mesh):
    wide = Mesh(mesh.devices.reshape(XS, ZS, -1), ("x", "z", "space"))
    in_specs = (P(("x", "z"), None, "space", None), P(("x", "z")), P("space", None))
    out_specs = P(("x", "z"), None, "space", None)
    return jax.shard_map(
        per_device, mesh=wide, in_specs=in_specs, out_specs=out_specs, check_vma=False
    )
```

```python
import functools

import jax
import jax.numpy as jnp
from jax import lax
from jax.experimental import pallas as pl
from jax.experimental.pallas import tpu as pltpu
from jax.sharding import Mesh, PartitionSpec as P

F32 = jnp.float32
XS, ZS = 4, 8
LANES = 128
BOXES = 10
VMEM = pl.BlockSpec(memory_space=pltpu.VMEM)
SMEM = pl.BlockSpec(memory_space=pltpu.SMEM)
PARAMS = pltpu.CompilerParams(vmem_limit_bytes=12 * 1024 * 1024)


def one_step(h, m, n, slope_x, slope_y):
    rows, cols = h.shape
    inv = 1.0 / h
    u = m * inv
    press = 0.0625 * (h * h)
    fx = 0.125 * (m * u) + press
    cross = 0.125 * (u * n)
    gy = 0.125 * (n * (n * inv)) + press

    def combine(q, f, g):
        q = 0.25 * q
        return (
            pltpu.roll(q - f, cols - 1, 1)
            + pltpu.roll(q + f, 1, 1)
            + pltpu.roll(q - g, rows - 1, 0)
            + pltpu.roll(q + g, 1, 0)
        )

    return (
        combine(h, 0.125 * m, 0.125 * n),
        combine(m, fx, cross) + h * slope_x,
        combine(n, cross, gy) + h * slope_y,
    )


def edge_kernel(counts_ref, x_ref, bed_ref, low_ref, high_ref, row_ref):
    count, fields, rows, _ = x_ref.shape
    for p in range(count):
        for f in range(fields):
            low_ref[p * fields + f] = x_ref[p, f, rows - 2 : rows]
            high_ref[p * fields + f] = x_ref[p, f, 0:2]
    low_ref[count * fields] = bed_ref[rows - 2 : rows]
    high_ref[count * fields] = bed_ref[0:2]
    lane = lax.broadcasted_iota(jnp.int32, (1, LANES), 1)
    total = jnp.int32(0)
    tile = jnp.zeros((1, LANES), jnp.int32)
    for j in range(count):
        c = counts_ref[j]
        total = total + c
        tile = jnp.where(lane == j, c, tile)
    tile = jnp.where(lane == count, total, tile)
    row_ref[...] = tile


def evolve_kernel(place_ref, x_ref, low_ref, high_ref, bed_ref, *refs):
    rows_ref, refs = refs[0:XS], refs[XS:]
    upper, lower = refs[0:XS], refs[XS : 2 * XS]
    row_ref, ext, sx, sy, res = refs[2 * XS :]
    count, fields, rows, cols = x_ref.shape
    ext[...] = jnp.ones_like(ext)
    ext[0, 0:rows] = bed_ref[...]
    ext[0, rows : rows + 2] = high_ref[count * fields]
    ext[0, rows + 6 : rows + 8] = low_ref[count * fields]
    b = ext[0]
    sx[...] = -0.125 * (pltpu.roll(b, cols - 1, 1) - pltpu.roll(b, 1, 1))
    sy[...] = -0.125 * (pltpu.roll(b, rows + 7, 0) - pltpu.roll(b, 1, 0))
    x = place_ref[0]

    def body(p, carry):
        for f in range(fields):
            ext[f, 0:rows] = x_ref[p, f]
            ext[f, rows : rows + 2] = high_ref[p * fields + f]
            ext[f, rows + 6 : rows + 8] = low_ref[p * fields + f]
        slope_x = sx[...]
        slope_y = sy[...]
        state = (ext[0], ext[1], ext[2])
        for _ in range(2):
            state = one_step(*state, slope_x, slope_y)
        for f in range(fields):
            res[f] = state[f][0:rows]
        for k in range(XS):
            at = pl.multiple_of(((x + k) % XS) * LANES, LANES)
            for f in range(fields):
                upper[k][p, f] = res[f, 0:8, pl.ds(at, LANES)]
                lower[k][p, f] = res[f, 8:16, pl.ds(at, LANES)]
        return carry

    lax.fori_loop(0, count, body, 0)
    for z in range(ZS):
        for k in range(XS):
            row_ref[z, k : k + 1] = rows_ref[k][...]


def plan_kernel(place_ref, row_ref, put_ref, take_ref, base, ctr):
    x, z = place_ref[0], place_ref[1]
    back = [(x + XS - k) % XS for k in range(XS)]
    total = jnp.int32(0)
    for at in range(XS):
        k = (x + XS - at) % XS
        for zs in range(ZS):
            base[at * ZS + zs] = total
            total = total + row_ref[zs, k, 16]
    base[XS * ZS] = total
    for i in range(ZS):
        ctr[i] = 0
    for i in range(16 * ZS):
        put_ref[i] = 0
    dump = 16 * ZS

    for k in range(XS):
        e = base[back[k] * ZS + z]
        for j in range(16):
            c = row_ref[z, k, j]
            for i in range(2):
                to = (e + i - z) & (ZS - 1)
                t = ctr[to]
                live = c > i
                ctr[to] = t + live.astype(jnp.int32)
                put_ref[jnp.where(live, to * 16 + t, dump)] = k * 16 + j
            e = e + c

    for i in range(ZS):
        ctr[i] = 0
    dump = 16 * XS
    for k in range(XS):
        for zs in range(ZS):
            lo = base[back[k] * ZS + zs]
            hi = base[back[k] * ZS + zs + 1]
            first = lo + ((z - lo) & (ZS - 1))
            t0 = ctr[zs]
            box = ((z - zs) & (ZS - 1)) * 16 + t0
            for i in range(4):
                s = first + i * ZS
                take_ref[jnp.where(s < hi, s >> 3, dump)] = box + i
            ctr[zs] = t0 + jnp.maximum((hi - first + ZS - 1) >> 3, 0)


def plan(place, row):
    return pl.pallas_call(
        plan_kernel,
        in_specs=[SMEM, SMEM],
        out_specs=[SMEM, SMEM],
        out_shape=[
            jax.ShapeDtypeStruct((16 * ZS + 8,), jnp.int32),
            jax.ShapeDtypeStruct((16 * XS + 8,), jnp.int32),
        ],
        scratch_shapes=[
            pltpu.SMEM((XS * ZS + 1,), jnp.int32),
            pltpu.SMEM((ZS,), jnp.int32),
        ],
        compiler_params=PARAMS,
        cost_estimate=pl.CostEstimate(flops=0, bytes_accessed=4_000_000, transcendentals=0),
    )(place, row)


def pick(parts, code):
    which, item = code >> 4, code & 15
    value = parts[0][item]
    for k in range(1, len(parts)):
        value = jnp.where(which == k, parts[k][item], value)
    return value


def pack_kernel(put_ref, *refs):
    data, outs = refs[0:XS], refs[XS:]
    for zs in range(ZS):

        def body(t, carry):
            outs[zs][t] = pick(data, put_ref[zs * 16 + t])
            return carry

        lax.fori_loop(0, BOXES, body, 0, unroll=5)


def pack(put, data):
    return pl.pallas_call(
        pack_kernel,
        in_specs=[SMEM] + [VMEM] * XS,
        out_specs=[VMEM] * ZS,
        out_shape=[jax.ShapeDtypeStruct((BOXES, 3, 8, LANES), F32)] * ZS,
        compiler_params=PARAMS,
        cost_estimate=pl.CostEstimate(flops=0, bytes_accessed=3_000_000, transcendentals=0),
    )(put, *data)


def spread_kernel(place_ref, take_ref, *refs):
    boxes, outs = refs[0:ZS], refs[ZS:]
    x = place_ref[0]
    for k in range(XS):
        to = (x + k) % XS

        def body(i, carry):
            code = take_ref[i * XS + to]
            outs[k][i] = pick(boxes, code)
            return carry

        lax.fori_loop(0, 16, body, 0, unroll=4)


def spread(place, take, boxes):
    return pl.pallas_call(
        spread_kernel,
        in_specs=[SMEM, SMEM] + [VMEM] * ZS,
        out_specs=[VMEM] * XS,
        out_shape=[jax.ShapeDtypeStruct((16, 3, 8, LANES), F32)] * XS,
        compiler_params=PARAMS,
        cost_estimate=pl.CostEstimate(flops=0, bytes_accessed=3_000_000, transcendentals=0),
    )(place, take, *boxes)


def join_kernel(place_ref, *refs):
    parts, out_ref = refs[: 2 * XS], refs[2 * XS]
    x = place_ref[0]
    for k in range(XS):
        at = pl.multiple_of(((x + XS - k) % XS) * LANES, LANES)

        def body(i, carry):
            for f in range(3):
                out_ref[i, f, 0:8, pl.ds(at, LANES)] = parts[k][i, f]
                out_ref[i, f, 8:16, pl.ds(at, LANES)] = parts[XS + k][i, f]
            return carry

        lax.fori_loop(0, 16, body, 0, unroll=4)


def along(axis, parts):
    n = len(parts)
    return [parts[0]] + [
        lax.ppermute(parts[k], axis, [(i, (i + k) % n) for i in range(n)]) for k in range(1, n)
    ]


def per_device(particles, counts, bed):
    count, fields, rows, cols = particles.shape
    place = jnp.stack([lax.axis_index("x"), lax.axis_index("z")]).astype(jnp.int32)
    edges = jax.ShapeDtypeStruct((count * fields + 1, 2, cols), F32)
    low, high, row = pl.pallas_call(
        edge_kernel,
        in_specs=[SMEM, VMEM, VMEM],
        out_specs=[VMEM] * 3,
        out_shape=[edges, edges, jax.ShapeDtypeStruct((1, LANES), jnp.int32)],
        compiler_params=PARAMS,
    )(counts, particles, bed)
    strips = lax.axis_size("space")
    low = lax.ppermute(low, "space", [(i, (i + 1) % strips) for i in range(strips)])
    high = lax.ppermute(high, "space", [((i + 1) % strips, i) for i in range(strips)])
    known = along("x", [row] * XS)
    half = jax.ShapeDtypeStruct((count, fields, 8, LANES), F32)
    *parts, row = pl.pallas_call(
        evolve_kernel,
        in_specs=[SMEM] + [VMEM] * (4 + XS),
        out_specs=[VMEM] * (2 * XS + 1),
        out_shape=[half] * (2 * XS) + [jax.ShapeDtypeStruct((ZS, XS, LANES), jnp.int32)],
        scratch_shapes=[
            pltpu.VMEM((fields, rows + 8, cols), F32),
            pltpu.VMEM((rows + 8, cols), F32),
            pltpu.VMEM((rows + 8, cols), F32),
            pltpu.VMEM((fields, rows, cols), F32),
        ],
        compiler_params=PARAMS,
        cost_estimate=pl.CostEstimate(flops=0, bytes_accessed=20_000_000, transcendentals=0),
    )(place, particles, low, high, bed, *known)
    upper = along("x", parts[:XS])
    row = lax.all_to_all(row, "z", 0, 0, tiled=True)
    lower = along("x", parts[XS:])
    put, take = plan(place, row)
    boxes_a = along("z", pack(put, upper))
    boxes_b = along("z", pack(put, lower))
    out_a = along("x", spread(place, take, boxes_a))
    out_b = along("x", spread(place, take, boxes_b))
    return pl.pallas_call(
        join_kernel,
        in_specs=[SMEM] + [VMEM] * (2 * XS),
        out_specs=VMEM,
        out_shape=jax.ShapeDtypeStruct(particles.shape, F32),
        compiler_params=PARAMS,
    )(place, *out_a, *out_b)


def solution(mesh):
    wide = Mesh(mesh.devices.reshape(XS, ZS, -1), ("x", "z", "space"))
    in_specs = (P(("x", "z"), None, "space", None), P(("x", "z")), P("space", None))
    out_specs = P(("x", "z"), None, "space", None)
    return jax.shard_map(
        per_device, mesh=wide, in_specs=in_specs, out_specs=out_specs, check_vma=False
    )
```

```python
import functools

import jax
import jax.numpy as jnp
from jax import lax
from jax.experimental import pallas as pl
from jax.experimental.pallas import tpu as pltpu
from jax.sharding import Mesh, PartitionSpec as P

F32 = jnp.float32
XS, ZS = 4, 8
LANES = 128
BOXES = 10
VMEM = pl.BlockSpec(memory_space=pltpu.VMEM)
SMEM = pl.BlockSpec(memory_space=pltpu.SMEM)
PARAMS = pltpu.CompilerParams(vmem_limit_bytes=12 * 1024 * 1024)


def one_step(h, m, n, slope_x, slope_y):
    rows, cols = h.shape
    inv = 1.0 / h
    u = m * inv
    press = 0.0625 * (h * h)
    fx = 0.125 * (m * u) + press
    cross = 0.125 * (u * n)
    gy = 0.125 * (n * (n * inv)) + press

    def combine(q, f, g):
        q = 0.25 * q
        return (
            pltpu.roll(q - f, cols - 1, 1)
            + pltpu.roll(q + f, 1, 1)
            + pltpu.roll(q - g, rows - 1, 0)
            + pltpu.roll(q + g, 1, 0)
        )

    return (
        combine(h, 0.125 * m, 0.125 * n),
        combine(m, fx, cross) + h * slope_x,
        combine(n, cross, gy) + h * slope_y,
    )


def edge_kernel(x_ref, bed_ref, low_ref, high_ref):
    count, fields, rows, _ = x_ref.shape
    for p in range(count):
        for f in range(fields):
            low_ref[p * fields + f] = x_ref[p, f, rows - 2 : rows]
            high_ref[p * fields + f] = x_ref[p, f, 0:2]
    low_ref[count * fields] = bed_ref[rows - 2 : rows]
    high_ref[count * fields] = bed_ref[0:2]


def evolve_kernel(place_ref, counts_ref, x_ref, low_ref, high_ref, bed_ref, *refs):
    upper, lower = refs[0:XS], refs[XS : 2 * XS]
    row_ref, ext, sx, sy, res = refs[2 * XS :]
    count, fields, rows, cols = x_ref.shape
    ext[...] = jnp.ones_like(ext)
    ext[0, 0:rows] = bed_ref[...]
    ext[0, rows : rows + 2] = high_ref[count * fields]
    ext[0, rows + 6 : rows + 8] = low_ref[count * fields]
    b = ext[0]
    sx[...] = -0.125 * (pltpu.roll(b, cols - 1, 1) - pltpu.roll(b, 1, 1))
    sy[...] = -0.125 * (pltpu.roll(b, rows + 7, 0) - pltpu.roll(b, 1, 0))
    x = place_ref[0]

    def body(p, carry):
        for f in range(fields):
            ext[f, 0:rows] = x_ref[p, f]
            ext[f, rows : rows + 2] = high_ref[p * fields + f]
            ext[f, rows + 6 : rows + 8] = low_ref[p * fields + f]
        slope_x = sx[...]
        slope_y = sy[...]
        state = (ext[0], ext[1], ext[2])
        for _ in range(2):
            state = one_step(*state, slope_x, slope_y)
        for f in range(fields):
            res[f] = state[f][0:rows]
        for k in range(XS):
            at = pl.multiple_of(((x + k) % XS) * LANES, LANES)
            for f in range(fields):
                upper[k][p, f] = res[f, 0:8, pl.ds(at, LANES)]
                lower[k][p, f] = res[f, 8:16, pl.ds(at, LANES)]
        return carry

    lax.fori_loop(0, count, body, 0)
    lane = lax.broadcasted_iota(jnp.int32, (1, LANES), 1)
    total = jnp.int32(0)
    tile = jnp.zeros((1, LANES), jnp.int32)
    for j in range(count):
        c = counts_ref[j]
        total = total + c
        tile = jnp.where(lane == j, c, tile)
    tile = jnp.where(lane == count, total, tile)
    for g in range(XS * ZS):
        row_ref[g] = tile


def send_plan_kernel(place_ref, row_ref, put_ref, base_ref, ctr):
    x, z = place_ref[0], place_ref[1]
    total = jnp.int32(0)
    for g in range(XS * ZS):
        base_ref[g] = total
        total = total + row_ref[g, 0, 16]
    base_ref[XS * ZS] = total
    for i in range(ZS):
        ctr[i] = 0
    for i in range(16 * ZS):
        put_ref[i] = 0
    dump = 16 * ZS
    for k in range(XS):
        group = ((x + XS - k) % XS) * ZS + z
        e = base_ref[group]
        for j in range(16):
            c = row_ref[group, 0, j]
            for i in range(2):
                to = (e + i - z) & (ZS - 1)
                t = ctr[to]
                live = c > i
                ctr[to] = t + live.astype(jnp.int32)
                put_ref[jnp.where(live, to * 16 + t, dump)] = k * 16 + j
            e = e + c


def take_plan_kernel(place_ref, base_ref, take_ref, ctr):
    x, z = place_ref[0], place_ref[1]
    for i in range(ZS):
        ctr[i] = 0
    dump = 16 * XS
    for k in range(XS):
        for zs in range(ZS):
            group = ((x + XS - k) % XS) * ZS + zs
            lo = base_ref[group]
            hi = base_ref[group + 1]
            first = lo + ((z - lo) & (ZS - 1))
            t0 = ctr[zs]
            box = ((z - zs) & (ZS - 1)) * 16 + t0
            for i in range(4):
                s = first + i * ZS
                take_ref[jnp.where(s < hi, s >> 3, dump)] = box + i
            ctr[zs] = t0 + jnp.maximum((hi - first + ZS - 1) >> 3, 0)


def send_plan(place, row):
    return pl.pallas_call(
        send_plan_kernel,
        in_specs=[SMEM, SMEM],
        out_specs=[SMEM, SMEM],
        out_shape=[
            jax.ShapeDtypeStruct((16 * ZS + 8,), jnp.int32),
            jax.ShapeDtypeStruct((XS * ZS + 8,), jnp.int32),
        ],
        scratch_shapes=[pltpu.SMEM((ZS,), jnp.int32)],
        compiler_params=PARAMS,
        cost_estimate=pl.CostEstimate(flops=0, bytes_accessed=4_000_000, transcendentals=0),
    )(place, row)


def take_plan(place, base):
    return pl.pallas_call(
        take_plan_kernel,
        in_specs=[SMEM, SMEM],
        out_specs=SMEM,
        out_shape=jax.ShapeDtypeStruct((16 * XS + 8,), jnp.int32),
        scratch_shapes=[pltpu.SMEM((ZS,), jnp.int32)],
        compiler_params=PARAMS,
        cost_estimate=pl.CostEstimate(flops=0, bytes_accessed=4_000_000, transcendentals=0),
    )(place, base)


def pick(parts, code):
    which, item = code >> 4, code & 15
    value = parts[0][item]
    for k in range(1, len(parts)):
        value = jnp.where(which == k, parts[k][item], value)
    return value


def pack_kernel(put_ref, *refs):
    data, outs = refs[0:XS], refs[XS:]
    for zs in range(ZS):

        def body(t, carry):
            outs[zs][t] = pick(data, put_ref[zs * 16 + t])
            return carry

        lax.fori_loop(0, BOXES, body, 0, unroll=5)


def pack(put, data):
    return pl.pallas_call(
        pack_kernel,
        in_specs=[SMEM] + [VMEM] * XS,
        out_specs=[VMEM] * ZS,
        out_shape=[jax.ShapeDtypeStruct((BOXES, 3, 8, LANES), F32)] * ZS,
        compiler_params=PARAMS,
        cost_estimate=pl.CostEstimate(flops=0, bytes_accessed=3_000_000, transcendentals=0),
    )(put, *data)


def pack_whole_kernel(place_ref, put_ref, *refs):
    data, out = refs[0:XS], refs[XS]
    z = place_ref[1]
    for k in range(ZS):
        to = (z + k) & (ZS - 1)

        def body(t, carry):
            out[to, t] = pick(data, put_ref[k * 16 + t])
            return carry

        lax.fori_loop(0, BOXES, body, 0, unroll=5)


def pack_whole(place, put, data):
    return pl.pallas_call(
        pack_whole_kernel,
        in_specs=[SMEM] * 2 + [VMEM] * XS,
        out_specs=VMEM,
        out_shape=jax.ShapeDtypeStruct((ZS, BOXES, 3, 8, LANES), F32),
        compiler_params=PARAMS,
        cost_estimate=pl.CostEstimate(flops=0, bytes_accessed=3_000_000, transcendentals=0),
    )(place, put, *data)


def spread_whole_kernel(place_ref, take_ref, boxes, *outs):
    x, z = place_ref[0], place_ref[1]
    for i in range(16 * XS):
        outs[XS][i] = take_ref[i]
    for k in range(XS):
        to = (x + k) % XS

        def body(i, carry):
            code = take_ref[i * XS + to]
            outs[k][i] = boxes[(z - (code >> 4)) & (ZS - 1), code & 15]
            return carry

        lax.fori_loop(0, 16, body, 0, unroll=4)


def spread_whole(place, take, boxes):
    return pl.pallas_call(
        spread_whole_kernel,
        in_specs=[SMEM, SMEM, VMEM],
        out_specs=[VMEM] * XS + [SMEM],
        out_shape=[jax.ShapeDtypeStruct((16, 3, 8, LANES), F32)] * XS
        + [jax.ShapeDtypeStruct((16 * XS,), jnp.int32)],
        compiler_params=PARAMS,
        cost_estimate=pl.CostEstimate(flops=0, bytes_accessed=3_000_000, transcendentals=0),
    )(place, take, boxes)


def spread_kernel(place_ref, take_ref, *refs):
    boxes, outs = refs[0:ZS], refs[ZS:]
    x = place_ref[0]
    for k in range(XS):
        to = (x + k) % XS

        def body(i, carry):
            code = take_ref[i * XS + to]
            outs[k][i] = pick(boxes, code)
            return carry

        lax.fori_loop(0, 16, body, 0, unroll=4)


def spread(place, take, boxes):
    return pl.pallas_call(
        spread_kernel,
        in_specs=[SMEM, SMEM] + [VMEM] * ZS,
        out_specs=[VMEM] * XS,
        out_shape=[jax.ShapeDtypeStruct((16, 3, 8, LANES), F32)] * XS,
        compiler_params=PARAMS,
        cost_estimate=pl.CostEstimate(flops=0, bytes_accessed=3_000_000, transcendentals=0),
    )(place, take, *boxes)


def join_kernel(place_ref, *refs):
    parts, out_ref = refs[: 2 * XS], refs[2 * XS]
    x = place_ref[0]
    for k in range(XS):
        at = pl.multiple_of(((x + XS - k) % XS) * LANES, LANES)

        def body(i, carry):
            for f in range(3):
                out_ref[i, f, 0:8, pl.ds(at, LANES)] = parts[k][i, f]
                out_ref[i, f, 8:16, pl.ds(at, LANES)] = parts[XS + k][i, f]
            return carry

        lax.fori_loop(0, 16, body, 0, unroll=4)


def along(axis, parts):
    n = len(parts)
    return [parts[0]] + [
        lax.ppermute(parts[k], axis, [(i, (i + k) % n) for i in range(n)]) for k in range(1, n)
    ]


def per_device(particles, counts, bed):
    count, fields, rows, cols = particles.shape
    place = jnp.stack([lax.axis_index("x"), lax.axis_index("z")]).astype(jnp.int32)
    edges = jax.ShapeDtypeStruct((count * fields + 1, 2, cols), F32)
    low, high = pl.pallas_call(
        edge_kernel,
        in_specs=[VMEM, VMEM],
        out_specs=[VMEM] * 2,
        out_shape=[edges, edges],
        compiler_params=PARAMS,
    )(particles, bed)
    strips = lax.axis_size("space")
    low = lax.ppermute(low, "space", [(i, (i + 1) % strips) for i in range(strips)])
    high = lax.ppermute(high, "space", [((i + 1) % strips, i) for i in range(strips)])
    half = jax.ShapeDtypeStruct((count, fields, 8, LANES), F32)
    *parts, row = pl.pallas_call(
        evolve_kernel,
        in_specs=[SMEM] * 2 + [VMEM] * 4,
        out_specs=[VMEM] * (2 * XS + 1),
        out_shape=[half] * (2 * XS) + [jax.ShapeDtypeStruct((XS * ZS, 1, LANES), jnp.int32)],
        scratch_shapes=[
            pltpu.VMEM((fields, rows + 8, cols), F32),
            pltpu.VMEM((rows + 8, cols), F32),
            pltpu.VMEM((rows + 8, cols), F32),
            pltpu.VMEM((fields, rows, cols), F32),
        ],
        compiler_params=PARAMS,
        cost_estimate=pl.CostEstimate(flops=0, bytes_accessed=20_000_000, transcendentals=0),
    )(place, counts, particles, low, high, bed)
    upper = along("x", parts[:XS])
    row = lax.all_to_all(row, ("x", "z"), 0, 0, tiled=True)
    lower = along("x", parts[XS:])
    put, base = send_plan(place, row)
    boxes_a = lax.all_to_all(pack_whole(place, put, upper), "z", 0, 0, tiled=True)
    boxes_b = along("z", pack(put, lower))
    take = take_plan(place, base)
    *out_a, take = spread_whole(place, take, boxes_a)
    out_a = along("x", out_a)
    out_b = along("x", spread(place, take, boxes_b))
    return pl.pallas_call(
        join_kernel,
        in_specs=[SMEM] + [VMEM] * (2 * XS),
        out_specs=VMEM,
        out_shape=jax.ShapeDtypeStruct(particles.shape, F32),
        compiler_params=PARAMS,
    )(place, *out_a, *out_b)


def solution(mesh):
    wide = Mesh(mesh.devices.reshape(XS, ZS, -1), ("x", "z", "space"))
    in_specs = (P(("x", "z"), None, "space", None), P(("x", "z")), P("space", None))
    out_specs = P(("x", "z"), None, "space", None)
    return jax.shard_map(
        per_device, mesh=wide, in_specs=in_specs, out_specs=out_specs, check_vma=False
    )
```

```python
import jax
import jax.numpy as jnp
from jax import lax
from jax.experimental import pallas as pl
from jax.experimental.pallas import tpu as pltpu
from jax.sharding import PartitionSpec as P

F32 = jnp.float32
LANES = 128
VMEM = pl.BlockSpec(memory_space=pltpu.VMEM)
SMEM = pl.BlockSpec(memory_space=pltpu.SMEM)
PARAMS = pltpu.CompilerParams(vmem_limit_bytes=12 * 1024 * 1024)


def one_step(h, m, n, slope_x, slope_y):
    rows, cols = h.shape
    inv = 1.0 / h
    u = m * inv
    press = 0.0625 * (h * h)
    fx = 0.125 * (m * u) + press
    cross = 0.125 * (u * n)
    gy = 0.125 * (n * (n * inv)) + press

    def combine(q, f, g):
        q = 0.25 * q
        return (
            pltpu.roll(q - f, cols - 1, 1)
            + pltpu.roll(q + f, 1, 1)
            + pltpu.roll(q - g, rows - 1, 0)
            + pltpu.roll(q + g, 1, 0)
        )

    return (
        combine(h, 0.125 * m, 0.125 * n),
        combine(m, fx, cross) + h * slope_x,
        combine(n, cross, gy) + h * slope_y,
    )


def edge_kernel(x_ref, bed_ref, low_ref, high_ref):
    count, fields, rows, _ = x_ref.shape
    for p in range(count):
        for f in range(fields):
            low_ref[p * fields + f] = x_ref[p, f, rows - 2 : rows]
            high_ref[p * fields + f] = x_ref[p, f, 0:2]
    low_ref[count * fields] = bed_ref[rows - 2 : rows]
    high_ref[count * fields] = bed_ref[0:2]


def row_kernel(counts_ref, row_ref):
    total = counts_ref[0]
    for j in range(1, counts_ref.shape[0]):
        total = total + counts_ref[j]
    row_ref[...] = jnp.full(row_ref.shape, total, jnp.int32)


def evolve_kernel(x_ref, low_ref, high_ref, bed_ref, out_ref, token_ref, ext, sx, sy):
    count, fields, rows, cols = x_ref.shape
    ext[...] = jnp.ones_like(ext)
    ext[0, 0:rows] = bed_ref[...]
    ext[0, rows : rows + 2] = high_ref[count * fields]
    ext[0, rows + 6 : rows + 8] = low_ref[count * fields]
    b = ext[0]
    sx[...] = -0.125 * (pltpu.roll(b, cols - 1, 1) - pltpu.roll(b, 1, 1))
    sy[...] = -0.125 * (pltpu.roll(b, rows + 7, 0) - pltpu.roll(b, 1, 0))

    def body(p, carry):
        for f in range(fields):
            ext[f, 0:rows] = x_ref[p, f]
            ext[f, rows : rows + 2] = high_ref[p * fields + f]
            ext[f, rows + 6 : rows + 8] = low_ref[p * fields + f]
        slope_x = sx[...]
        slope_y = sy[...]
        state = (ext[0], ext[1], ext[2])
        for _ in range(2):
            state = one_step(*state, slope_x, slope_y)
        for f in range(fields):
            out_ref[p, f] = state[f][0:rows]
        return carry

    lax.fori_loop(0, count, body, 0)
    token_ref[0] = 0


def pack_kernel(place_ref, token_ref, counts_ref, row_ref, done_ref, out_ref, entry_ref, source):
    groups = row_ref.shape[0]
    count = counts_ref.shape[0]
    me = place_ref[0]
    for r in range(groups + 1):
        source[r] = 0
    for k in range(count):
        entry_ref[k] = 0
    total = jnp.int32(0)
    mine = jnp.int32(0)
    for g in range(groups):
        mine = jnp.where(me == g, total, mine)
        later = total + row_ref[g, 0, 0]
        k = (total - me + groups - 1) // groups
        entry_ref[jnp.where(k * groups + me < later, k, count)] = g
        total = later
    e = mine
    for p in range(count):
        c = counts_ref[p]
        source[jnp.where(c > 0, e & (groups - 1), groups)] = p
        source[jnp.where(c > 1, (e + 1) & (groups - 1), groups)] = p
        e = e + c

    def body(r, carry):
        out_ref[r] = done_ref[source[r]]
        return carry

    lax.fori_loop(0, groups, body, 0, unroll=2)


def unpack_kernel(entry_ref, parcel_ref, out_ref, sem):
    count = out_ref.shape[0]
    copies = [
        pltpu.make_async_copy(parcel_ref.at[entry_ref[k]], out_ref.at[k], sem.at[k])
        for k in range(count)
    ]
    for copy in copies:
        copy.start()
    for copy in copies:
        copy.wait()


def per_device(particles, counts, bed):
    count, fields, rows, cols = particles.shape
    groups = lax.axis_size("dom")
    place = lax.axis_index("dom").astype(jnp.int32)[None]
    edges = jax.ShapeDtypeStruct((count * fields + 1, 2, cols), F32)
    row = pl.pallas_call(
        row_kernel,
        in_specs=[SMEM],
        out_specs=VMEM,
        out_shape=jax.ShapeDtypeStruct((groups, 1, LANES), jnp.int32),
        compiler_params=PARAMS,
    )(counts)
    row = lax.all_to_all(row, "dom", 0, 0, tiled=True)
    low, high = pl.pallas_call(
        edge_kernel,
        in_specs=[VMEM, VMEM],
        out_specs=[VMEM] * 2,
        out_shape=[edges, edges],
        compiler_params=PARAMS,
    )(particles, bed)
    strips = lax.axis_size("space")
    low = lax.ppermute(low, "space", [(i, (i + 1) % strips) for i in range(strips)])
    high = lax.ppermute(high, "space", [((i + 1) % strips, i) for i in range(strips)])
    done, token = pl.pallas_call(
        evolve_kernel,
        in_specs=[VMEM] * 4,
        out_specs=[VMEM, SMEM],
        out_shape=[
            jax.ShapeDtypeStruct(particles.shape, F32),
            jax.ShapeDtypeStruct((1,), jnp.int32),
        ],
        scratch_shapes=[
            pltpu.VMEM((fields, rows + 8, cols), F32),
            pltpu.VMEM((rows + 8, cols), F32),
            pltpu.VMEM((rows + 8, cols), F32),
        ],
        compiler_params=PARAMS,
        cost_estimate=pl.CostEstimate(flops=0, bytes_accessed=20_000_000, transcendentals=0),
    )(particles, low, high, bed)
    any_spec = pl.BlockSpec(memory_space=pl.ANY)
    parcel, entry = pl.pallas_call(
        pack_kernel,
        in_specs=[SMEM] * 4 + [VMEM],
        out_specs=[VMEM, SMEM],
        out_shape=[
            jax.ShapeDtypeStruct((groups,) + particles.shape[1:], F32),
            jax.ShapeDtypeStruct((count + 8,), jnp.int32),
        ],
        scratch_shapes=[pltpu.SMEM((groups + 8,), jnp.int32)],
        compiler_params=PARAMS,
        cost_estimate=pl.CostEstimate(flops=0, bytes_accessed=5_000_000, transcendentals=0),
    )(place, token, counts, row, done)
    parcel = lax.all_to_all(parcel, "dom", 0, 0, tiled=True)
    return pl.pallas_call(
        unpack_kernel,
        in_specs=[SMEM, any_spec],
        out_specs=any_spec,
        out_shape=jax.ShapeDtypeStruct(particles.shape, F32),
        scratch_shapes=[pltpu.SemaphoreType.DMA((count,))],
        compiler_params=PARAMS,
    )(entry, parcel)


def solution(mesh):
    in_specs = (P("dom", None, "space", None), P("dom"), P("space", None))
    out_specs = P("dom", None, "space", None)
    return jax.shard_map(
        per_device, mesh=mesh, in_specs=in_specs, out_specs=out_specs, check_vma=False
    )
```

```python
import jax
import jax.numpy as jnp
from jax import lax
from jax.experimental import pallas as pl
from jax.experimental.pallas import tpu as pltpu
from jax.sharding import PartitionSpec as P

F32 = jnp.float32
LANES = 128
PAIR = 4
VMEM = pl.BlockSpec(memory_space=pltpu.VMEM)
SMEM = pl.BlockSpec(memory_space=pltpu.SMEM)
PARAMS = pltpu.CompilerParams(vmem_limit_bytes=12 * 1024 * 1024)


def one_step(h, m, n, slope_x, slope_y):
    rows, cols = h.shape
    inv = 1.0 / h
    u = m * inv
    press = 0.0625 * (h * h)
    fx = 0.125 * (m * u) + press
    cross = 0.125 * (u * n)
    gy = 0.125 * (n * (n * inv)) + press

    def combine(q, f, g):
        q = 0.25 * q
        return (
            pltpu.roll(q - f, cols - 1, 1)
            + pltpu.roll(q + f, 1, 1)
            + pltpu.roll(q - g, rows - 1, 0)
            + pltpu.roll(q + g, 1, 0)
        )

    return (
        combine(h, 0.125 * m, 0.125 * n),
        combine(m, fx, cross) + h * slope_x,
        combine(n, cross, gy) + h * slope_y,
    )


def edge_kernel(x_ref, bed_ref, low_ref, high_ref):
    count, fields, rows, _ = x_ref.shape
    for p in range(count):
        for f in range(fields):
            low_ref[p * fields + f] = x_ref[p, f, rows - 2 : rows]
            high_ref[p * fields + f] = x_ref[p, f, 0:2]
    low_ref[count * fields] = bed_ref[rows - 2 : rows]
    high_ref[count * fields] = bed_ref[0:2]


def row_kernel(counts_ref, row_ref):
    total = counts_ref[0]
    for j in range(1, counts_ref.shape[0]):
        total = total + counts_ref[j]
    row_ref[...] = jnp.full(row_ref.shape, total, jnp.int32)


def evolve_kernel(x_ref, low_ref, high_ref, bed_ref, out_ref, token_ref, ext, sx, sy):
    count, fields, rows, cols = x_ref.shape
    ext[...] = jnp.ones_like(ext)
    ext[0, 0:rows] = bed_ref[...]
    ext[0, rows : rows + 2] = high_ref[count * fields]
    ext[0, rows + 6 : rows + 8] = low_ref[count * fields]
    b = ext[0]
    sx[...] = -0.125 * (pltpu.roll(b, cols - 1, 1) - pltpu.roll(b, 1, 1))
    sy[...] = -0.125 * (pltpu.roll(b, rows + 7, 0) - pltpu.roll(b, 1, 0))

    def one(p, at):
        for f in range(fields):
            ext[at + f, 0:rows] = x_ref[p, f]
            ext[at + f, rows : rows + 2] = high_ref[p * fields + f]
            ext[at + f, rows + 6 : rows + 8] = low_ref[p * fields + f]
        slope_x = sx[...]
        slope_y = sy[...]
        state = (ext[at], ext[at + 1], ext[at + 2])
        for _ in range(2):
            state = one_step(*state, slope_x, slope_y)
        for f in range(fields):
            out_ref[p, f] = state[f][0:rows]

    def body(i, carry):
        for j in range(PAIR):
            one(i * PAIR + j, j * fields)
        return carry

    lax.fori_loop(0, count // PAIR, body, 0)
    token_ref[0] = 0


def pack_kernel(place_ref, token_ref, counts_ref, row_ref, done_ref, out_ref, entry_ref, source):
    groups = row_ref.shape[0]
    count = counts_ref.shape[0]
    me = place_ref[0]
    shift = groups.bit_length() - 1
    for r in range(groups + 1):
        source[r] = 0
    total = jnp.int32(0)
    mine = jnp.int32(0)
    for g in range(groups):
        mine = jnp.where(me == g, total, mine)
        later = total + row_ref[g, 0, 0]
        k = (total - me + groups - 1) >> shift
        entry_ref[jnp.where(k * groups + me < later, k, count)] = g
        total = later
    e = mine
    for p in range(count):
        c = counts_ref[p]
        source[jnp.where(c > 0, e & (groups - 1), groups)] = p
        source[jnp.where(c > 1, (e + 1) & (groups - 1), groups)] = p
        e = e + c

    def body(r, carry):
        out_ref[r] = done_ref[source[r]]
        return carry

    lax.fori_loop(0, groups, body, 0, unroll=2)


def unpack_kernel(entry_ref, parcel_ref, out_ref, sem):
    count = out_ref.shape[0]
    copies = [
        pltpu.make_async_copy(parcel_ref.at[entry_ref[k]], out_ref.at[k], sem.at[k])
        for k in range(count)
    ]
    for copy in copies:
        copy.start()
    for copy in copies:
        copy.wait()


def per_device(particles, counts, bed):
    count, fields, rows, cols = particles.shape
    groups = lax.axis_size("dom")
    place = lax.axis_index("dom").astype(jnp.int32)[None]
    edges = jax.ShapeDtypeStruct((count * fields + 1, 2, cols), F32)
    row = pl.pallas_call(
        row_kernel,
        in_specs=[SMEM],
        out_specs=VMEM,
        out_shape=jax.ShapeDtypeStruct((groups, 1, LANES), jnp.int32),
        compiler_params=PARAMS,
    )(counts)
    row = lax.all_to_all(row, "dom", 0, 0, tiled=True)
    low, high = pl.pallas_call(
        edge_kernel,
        in_specs=[VMEM, VMEM],
        out_specs=[VMEM] * 2,
        out_shape=[edges, edges],
        compiler_params=PARAMS,
    )(particles, bed)
    strips = lax.axis_size("space")
    low = lax.ppermute(low, "space", [(i, (i + 1) % strips) for i in range(strips)])
    high = lax.ppermute(high, "space", [((i + 1) % strips, i) for i in range(strips)])
    done, token = pl.pallas_call(
        evolve_kernel,
        in_specs=[VMEM] * 4,
        out_specs=[VMEM, SMEM],
        out_shape=[
            jax.ShapeDtypeStruct(particles.shape, F32),
            jax.ShapeDtypeStruct((1,), jnp.int32),
        ],
        scratch_shapes=[
            pltpu.VMEM((PAIR * fields, rows + 8, cols), F32),
            pltpu.VMEM((rows + 8, cols), F32),
            pltpu.VMEM((rows + 8, cols), F32),
        ],
        compiler_params=PARAMS,
        cost_estimate=pl.CostEstimate(flops=0, bytes_accessed=20_000_000, transcendentals=0),
    )(particles, low, high, bed)
    any_spec = pl.BlockSpec(memory_space=pl.ANY)
    parcel, entry = pl.pallas_call(
        pack_kernel,
        in_specs=[SMEM] * 4 + [VMEM],
        out_specs=[VMEM, SMEM],
        out_shape=[
            jax.ShapeDtypeStruct((groups,) + particles.shape[1:], F32),
            jax.ShapeDtypeStruct((count + 8,), jnp.int32),
        ],
        scratch_shapes=[pltpu.SMEM((groups + 8,), jnp.int32)],
        compiler_params=PARAMS,
        cost_estimate=pl.CostEstimate(flops=0, bytes_accessed=5_000_000, transcendentals=0),
    )(place, token, counts, row, done)
    parcel = lax.all_to_all(parcel, "dom", 0, 0, tiled=True)
    return pl.pallas_call(
        unpack_kernel,
        in_specs=[SMEM, any_spec],
        out_specs=any_spec,
        out_shape=jax.ShapeDtypeStruct(particles.shape, F32),
        scratch_shapes=[pltpu.SemaphoreType.DMA((count,))],
        compiler_params=PARAMS,
    )(entry, parcel)


def solution(mesh):
    in_specs = (P("dom", None, "space", None), P("dom"), P("space", None))
    out_specs = P("dom", None, "space", None)
    return jax.shard_map(
        per_device, mesh=mesh, in_specs=in_specs, out_specs=out_specs, check_vma=False
    )
```

```python
import jax
import jax.numpy as jnp
from jax import lax
from jax.experimental import pallas as pl
from jax.experimental.pallas import tpu as pltpu
from jax.sharding import PartitionSpec as P

F32 = jnp.float32
LANES = 128
PAIR = 4
VMEM = pl.BlockSpec(memory_space=pltpu.VMEM)
SMEM = pl.BlockSpec(memory_space=pltpu.SMEM)
PARAMS = pltpu.CompilerParams(vmem_limit_bytes=12 * 1024 * 1024)


def one_step(h, m, n, slope_x, slope_y):
    rows, cols = h.shape
    inv = 1.0 / h
    u = m * inv
    press = 0.0625 * (h * h)
    fx = 0.125 * (m * u) + press
    cross = 0.125 * (u * n)
    gy = 0.125 * (n * (n * inv)) + press

    def combine(q, f, g):
        q = 0.25 * q
        return (
            pltpu.roll(q - f, cols - 1, 1)
            + pltpu.roll(q + f, 1, 1)
            + pltpu.roll(q - g, rows - 1, 0)
            + pltpu.roll(q + g, 1, 0)
        )

    return (
        combine(h, 0.125 * m, 0.125 * n),
        combine(m, fx, cross) + h * slope_x,
        combine(n, cross, gy) + h * slope_y,
    )


def edge_kernel(counts_ref, x_ref, bed_ref, low_ref, high_ref, row_ref):
    count, fields, rows, _ = x_ref.shape
    for p in range(count):
        for f in range(fields):
            low_ref[p * fields + f] = x_ref[p, f, rows - 2 : rows]
            high_ref[p * fields + f] = x_ref[p, f, 0:2]
    low_ref[count * fields] = bed_ref[rows - 2 : rows]
    high_ref[count * fields] = bed_ref[0:2]
    total = counts_ref[0]
    for j in range(1, count):
        total = total + counts_ref[j]
    row_ref[...] = jnp.full(row_ref.shape, total, jnp.int32)


def evolve_kernel(x_ref, low_ref, high_ref, bed_ref, out_ref, token_ref, ext, sx, sy):
    count, fields, rows, cols = x_ref.shape
    ext[...] = jnp.ones_like(ext)
    ext[0, 0:rows] = bed_ref[...]
    ext[0, rows : rows + 2] = high_ref[count * fields]
    ext[0, rows + 6 : rows + 8] = low_ref[count * fields]
    b = ext[0]
    sx[...] = -0.125 * (pltpu.roll(b, cols - 1, 1) - pltpu.roll(b, 1, 1))
    sy[...] = -0.125 * (pltpu.roll(b, rows + 7, 0) - pltpu.roll(b, 1, 0))

    def one(p, at):
        for f in range(fields):
            ext[at + f, 0:rows] = x_ref[p, f]
            ext[at + f, rows : rows + 2] = high_ref[p * fields + f]
            ext[at + f, rows + 6 : rows + 8] = low_ref[p * fields + f]
        slope_x = sx[...]
        slope_y = sy[...]
        state = (ext[at], ext[at + 1], ext[at + 2])
        for _ in range(2):
            state = one_step(*state, slope_x, slope_y)
        for f in range(fields):
            out_ref[p, f] = state[f][0:rows]

    def body(i, carry):
        for j in range(PAIR):
            one(i * PAIR + j, j * fields)
        return carry

    lax.fori_loop(0, count // PAIR, body, 0)
    token_ref[0] = 0


def pack_kernel(place_ref, token_ref, counts_ref, row_ref, done_ref, out_ref, entry_ref, source):
    groups = row_ref.shape[0]
    count = counts_ref.shape[0]
    me = place_ref[0]
    shift = groups.bit_length() - 1
    for r in range(groups + 1):
        source[r] = 0
    total = jnp.int32(0)
    mine = jnp.int32(0)
    for g in range(groups):
        mine = jnp.where(me == g, total, mine)
        later = total + row_ref[g, 0, 0]
        k = (total - me + groups - 1) >> shift
        entry_ref[jnp.where(k * groups + me < later, k, count)] = g
        total = later
    e = mine
    for p in range(count):
        c = counts_ref[p]
        source[jnp.where(c > 0, e & (groups - 1), groups)] = p
        source[jnp.where(c > 1, (e + 1) & (groups - 1), groups)] = p
        e = e + c

    def body(r, carry):
        out_ref[r] = done_ref[source[r]]
        return carry

    lax.fori_loop(0, groups, body, 0, unroll=2)


def unpack_kernel(entry_ref, parcel_ref, out_ref, sem):
    count = out_ref.shape[0]
    copies = [
        pltpu.make_async_copy(parcel_ref.at[entry_ref[k]], out_ref.at[k], sem.at[k])
        for k in range(count)
    ]
    for copy in copies:
        copy.start()
    for copy in copies:
        copy.wait()


def per_device(particles, counts, bed):
    count, fields, rows, cols = particles.shape
    groups = lax.axis_size("dom")
    place = lax.axis_index("dom").astype(jnp.int32)[None]
    edges = jax.ShapeDtypeStruct((count * fields + 1, 2, cols), F32)
    low, high, row = pl.pallas_call(
        edge_kernel,
        in_specs=[SMEM, VMEM, VMEM],
        out_specs=[VMEM] * 3,
        out_shape=[edges, edges, jax.ShapeDtypeStruct((groups, 1, LANES), jnp.int32)],
        compiler_params=pltpu.CompilerParams(vmem_limit_bytes=60 * 1024 * 1024),
    )(counts, particles, bed)
    row = lax.all_to_all(row, "dom", 0, 0, tiled=True)
    strips = lax.axis_size("space")
    low = lax.ppermute(low, "space", [(i, (i + 1) % strips) for i in range(strips)])
    high = lax.ppermute(high, "space", [((i + 1) % strips, i) for i in range(strips)])
    done, token = pl.pallas_call(
        evolve_kernel,
        in_specs=[VMEM] * 4,
        out_specs=[VMEM, SMEM],
        out_shape=[
            jax.ShapeDtypeStruct(particles.shape, F32),
            jax.ShapeDtypeStruct((1,), jnp.int32),
        ],
        scratch_shapes=[
            pltpu.VMEM((PAIR * fields, rows + 8, cols), F32),
            pltpu.VMEM((rows + 8, cols), F32),
            pltpu.VMEM((rows + 8, cols), F32),
        ],
        compiler_params=PARAMS,
        cost_estimate=pl.CostEstimate(flops=0, bytes_accessed=20_000_000, transcendentals=0),
    )(particles, low, high, bed)
    any_spec = pl.BlockSpec(memory_space=pl.ANY)
    parcel, entry = pl.pallas_call(
        pack_kernel,
        in_specs=[SMEM] * 4 + [VMEM],
        out_specs=[VMEM, SMEM],
        out_shape=[
            jax.ShapeDtypeStruct((groups,) + particles.shape[1:], F32),
            jax.ShapeDtypeStruct((count + 8,), jnp.int32),
        ],
        scratch_shapes=[pltpu.SMEM((groups + 8,), jnp.int32)],
        compiler_params=PARAMS,
        cost_estimate=pl.CostEstimate(flops=0, bytes_accessed=5_000_000, transcendentals=0),
    )(place, token, counts, row, done)
    parcel = lax.all_to_all(parcel, "dom", 0, 0, tiled=True)
    return pl.pallas_call(
        unpack_kernel,
        in_specs=[SMEM, any_spec],
        out_specs=any_spec,
        out_shape=jax.ShapeDtypeStruct(particles.shape, F32),
        scratch_shapes=[pltpu.SemaphoreType.DMA((count,))],
        compiler_params=PARAMS,
    )(entry, parcel)


def solution(mesh):
    in_specs = (P("dom", None, "space", None), P("dom"), P("space", None))
    out_specs = P("dom", None, "space", None)
    return jax.shard_map(
        per_device, mesh=mesh, in_specs=in_specs, out_specs=out_specs, check_vma=False
    )
```

```python
import jax
import jax.numpy as jnp
from jax import lax
from jax.experimental import pallas as pl
from jax.experimental.pallas import tpu as pltpu
from jax.sharding import PartitionSpec as P

F32 = jnp.float32
LANES = 128
PAIR = 8
VMEM = pl.BlockSpec(memory_space=pltpu.VMEM)
SMEM = pl.BlockSpec(memory_space=pltpu.SMEM)
PARAMS = pltpu.CompilerParams(vmem_limit_bytes=12 * 1024 * 1024)


def one_step(h, m, n, slope_x, slope_y):
    rows, cols = h.shape
    inv = 1.0 / h
    u = m * inv
    press = 0.0625 * (h * h)
    fx = 0.125 * (m * u) + press
    cross = 0.125 * (u * n)
    gy = 0.125 * (n * (n * inv)) + press

    def combine(q, f, g):
        q = 0.25 * q
        return (
            pltpu.roll(q - f, cols - 1, 1)
            + pltpu.roll(q + f, 1, 1)
            + pltpu.roll(q - g, rows - 1, 0)
            + pltpu.roll(q + g, 1, 0)
        )

    return (
        combine(h, 0.125 * m, 0.125 * n),
        combine(m, fx, cross) + h * slope_x,
        combine(n, cross, gy) + h * slope_y,
    )


def edge_kernel(counts_ref, x_ref, bed_ref, low_ref, high_ref, row_ref):
    count, fields, rows, _ = x_ref.shape
    for p in range(count):
        for f in range(fields):
            low_ref[p * fields + f] = x_ref[p, f, rows - 2 : rows]
            high_ref[p * fields + f] = x_ref[p, f, 0:2]
    low_ref[count * fields] = bed_ref[rows - 2 : rows]
    high_ref[count * fields] = bed_ref[0:2]
    total = counts_ref[0]
    for j in range(1, count):
        total = total + counts_ref[j]
    row_ref[...] = jnp.full(row_ref.shape, total, jnp.int32)


def evolve_kernel(x_ref, low_ref, high_ref, bed_ref, out_ref, token_ref, ext, sx, sy):
    count, fields, rows, cols = x_ref.shape
    ext[...] = jnp.ones_like(ext)
    ext[0, 0:rows] = bed_ref[...]
    ext[0, rows : rows + 2] = high_ref[count * fields]
    ext[0, rows + 6 : rows + 8] = low_ref[count * fields]
    b = ext[0]
    sx[...] = -0.125 * (pltpu.roll(b, cols - 1, 1) - pltpu.roll(b, 1, 1))
    sy[...] = -0.125 * (pltpu.roll(b, rows + 7, 0) - pltpu.roll(b, 1, 0))

    def one(p, at):
        for f in range(fields):
            ext[at + f, 0:rows] = x_ref[p, f]
            ext[at + f, rows : rows + 2] = high_ref[p * fields + f]
            ext[at + f, rows + 6 : rows + 8] = low_ref[p * fields + f]
        slope_x = sx[...]
        slope_y = sy[...]
        state = (ext[at], ext[at + 1], ext[at + 2])
        for _ in range(2):
            state = one_step(*state, slope_x, slope_y)
        for f in range(fields):
            out_ref[p, f] = state[f][0:rows]

    def body(i, carry):
        for j in range(PAIR):
            one(i * PAIR + j, j * fields)
        return carry

    lax.fori_loop(0, count // PAIR, body, 0)
    token_ref[0] = 0


def pack_kernel(place_ref, token_ref, counts_ref, row_ref, done_ref, out_ref, entry_ref, source):
    groups = row_ref.shape[0]
    count = counts_ref.shape[0]
    me = place_ref[0]
    shift = groups.bit_length() - 1
    for r in range(groups + 1):
        source[r] = 0
    total = jnp.int32(0)
    mine = jnp.int32(0)
    for g in range(groups):
        mine = jnp.where(me == g, total, mine)
        later = total + row_ref[g, 0, 0]
        k = (total - me + groups - 1) >> shift
        entry_ref[jnp.where(k * groups + me < later, k, count)] = g
        total = later
    e = mine
    for p in range(count):
        c = counts_ref[p]
        source[jnp.where(c > 0, e & (groups - 1), groups)] = p
        source[jnp.where(c > 1, (e + 1) & (groups - 1), groups)] = p
        e = e + c

    def body(r, carry):
        out_ref[r] = done_ref[source[r]]
        return carry

    lax.fori_loop(0, groups, body, 0, unroll=2)


def unpack_kernel(entry_ref, parcel_ref, out_ref, sem):
    count = out_ref.shape[0]
    copies = [
        pltpu.make_async_copy(parcel_ref.at[entry_ref[k]], out_ref.at[k], sem.at[k])
        for k in range(count)
    ]
    for copy in copies:
        copy.start()
    for copy in copies:
        copy.wait()


def per_device(particles, counts, bed):
    count, fields, rows, cols = particles.shape
    groups = lax.axis_size("dom")
    place = lax.axis_index("dom").astype(jnp.int32)[None]
    edges = jax.ShapeDtypeStruct((count * fields + 1, 2, cols), F32)
    low, high, row = pl.pallas_call(
        edge_kernel,
        in_specs=[SMEM, VMEM, VMEM],
        out_specs=[VMEM] * 3,
        out_shape=[edges, edges, jax.ShapeDtypeStruct((groups, 1, LANES), jnp.int32)],
        compiler_params=pltpu.CompilerParams(vmem_limit_bytes=60 * 1024 * 1024),
    )(counts, particles, bed)
    row = lax.all_to_all(row, "dom", 0, 0, tiled=True)
    strips = lax.axis_size("space")
    low = lax.ppermute(low, "space", [(i, (i + 1) % strips) for i in range(strips)])
    high = lax.ppermute(high, "space", [((i + 1) % strips, i) for i in range(strips)])
    done, token = pl.pallas_call(
        evolve_kernel,
        in_specs=[VMEM] * 4,
        out_specs=[VMEM, SMEM],
        out_shape=[
            jax.ShapeDtypeStruct(particles.shape, F32),
            jax.ShapeDtypeStruct((1,), jnp.int32),
        ],
        scratch_shapes=[
            pltpu.VMEM((PAIR * fields, rows + 8, cols), F32),
            pltpu.VMEM((rows + 8, cols), F32),
            pltpu.VMEM((rows + 8, cols), F32),
        ],
        compiler_params=PARAMS,
        cost_estimate=pl.CostEstimate(flops=0, bytes_accessed=20_000_000, transcendentals=0),
    )(particles, low, high, bed)
    any_spec = pl.BlockSpec(memory_space=pl.ANY)
    parcel, entry = pl.pallas_call(
        pack_kernel,
        in_specs=[SMEM] * 4 + [VMEM],
        out_specs=[VMEM, SMEM],
        out_shape=[
            jax.ShapeDtypeStruct((groups,) + particles.shape[1:], F32),
            jax.ShapeDtypeStruct((count + 8,), jnp.int32),
        ],
        scratch_shapes=[pltpu.SMEM((groups + 8,), jnp.int32)],
        compiler_params=PARAMS,
        cost_estimate=pl.CostEstimate(flops=0, bytes_accessed=5_000_000, transcendentals=0),
    )(place, token, counts, row, done)
    parcel = lax.all_to_all(parcel, "dom", 0, 0, tiled=True)
    return pl.pallas_call(
        unpack_kernel,
        in_specs=[SMEM, any_spec],
        out_specs=any_spec,
        out_shape=jax.ShapeDtypeStruct(particles.shape, F32),
        scratch_shapes=[pltpu.SemaphoreType.DMA((count,))],
        compiler_params=PARAMS,
    )(entry, parcel)


def solution(mesh):
    in_specs = (P("dom", None, "space", None), P("dom"), P("space", None))
    out_specs = P("dom", None, "space", None)
    return jax.shard_map(
        per_device, mesh=mesh, in_specs=in_specs, out_specs=out_specs, check_vma=False
    )
```
